256 devices in a mesh: depth: 64 (over y, z, core), space: 4 (over x).
Axes of the slice: x: 4, y: 4, z: 8, core: 2. Of those that a mesh axis runs over, the one named last changes fastest.
Arguments:
- coarse_states: float32 [64, 32, 128, 128], P('depth', 'space'), may hold values from -6 to 6
- first_kernels: bfloat16 [256, 9, 128, 128], P('depth'), may hold values from -0.1875 to 0.1875
- second_kernels: bfloat16 [256, 9, 128, 128], P('depth'), may hold values from -0.1875 to 0.1875
- coarse_channel_gain: float32 [64, 128], replicated, may hold values from 0 to 1, as said below
Outputs:
- states: float32 [256, 32, 128, 128], P('depth', 'space')
- relaxed: float32 [64, 32, 128, 128], P('depth', 'space')
The draws below stay inside these ranges and needn't reach their ends.
Inputs may be any that keep to these rules, and one draw needn't show every extreme that they name: `coarse_channel_gain`: each entry is positive and at most 1.
All inputs are finite; a program needn't handle non-finite values.
Results may differ from the reference program's by a relative error of at most 0.01.
Values may be sent and summed in bfloat16 or wider, within the bound.
No kernel may reach another device: no remote copies, remote signals or barrier semaphores. Data moves between devices by JAX's collectives and lax.ppermute only.
A program may use at most 128 MiB of HBM per device.

```python
import jax
import jax.numpy as jnp
from jax import lax

C = 128
CF = 4
W = 128
COARSE_POINTS = 64
LAYERS = 256
H = 32


def draw_coarse_channel_gain(key, part):
    random_keys = [jax.random.fold_in(key, 101 + index) for index in range(7)]
    share = 0.5
    slow = jax.random.uniform(random_keys[0], (C,)) < share
    slow_rate = jnp.log(0.2) / COARSE_POINTS * jax.random.uniform(random_keys[1], (C,), jnp.float32, 0.3, 1.0)
    fast_rate = jnp.log(0.1) / jax.random.uniform(random_keys[2], (C,), jnp.float32, 4.0, 20.0)
    rate = jnp.where(slow, slow_rate, fast_rate)
    jitter = jax.random.uniform(random_keys[3], (COARSE_POINTS, 1), jnp.float32, 0.5, 1.5)
    relaxation_sweep = jax.random.uniform(random_keys[4], (COARSE_POINTS, 1)) < 3.0 / COARSE_POINTS
    multiplier = jnp.where(relaxation_sweep, jax.random.uniform(random_keys[5], (COARSE_POINTS, 1), jnp.float32, 0.5, 0.8), 1.0)
    return (jnp.exp(rate[None, :] * jitter) * multiplier).astype(jnp.float32)


def shard_levels(stream_key, extent, shards, low, high):
    loudness, own = 1.0, jax.random.fold_in(stream_key, 6)
    for axis_at, blocks in shards:
        heights = jnp.exp(jax.random.uniform(jax.random.fold_in(own, axis_at), (blocks,), jnp.float32, low / len(shards), high / len(shards)))
        loudness = loudness * jnp.repeat(heights, extent[axis_at] // blocks).reshape([-1 if axis == axis_at else 1 for axis in range(len(extent))])
    return loudness


def gaussian(stream_key, extent, scale, most, cuts=(), kind=jnp.bfloat16):
    values = jax.random.normal(stream_key, extent, jnp.float32) * scale
    if len(cuts) > 0:
        values = shard_levels(stream_key, extent, cuts, -0.22, 0.18) * values
    return jnp.clip(values, min=-most, max=most).astype(kind)


def setup_inputs(seed: int = 0) -> dict:
    streams_of = jax.random.split(jax.random.key(seed), 5)
    return {
        "coarse_states": gaussian(streams_of[0], (COARSE_POINTS, H, W, C), 1.0, 6.0, ((0, 64), (1, 4)), jnp.float32),
        "first_kernels": gaussian(streams_of[1], (LAYERS, 9, C, C), (9 * C) ** -0.5, 0.1875, ((0, 64),)),
        "second_kernels": gaussian(streams_of[2], (LAYERS, 9, C, C), (9 * C) ** -0.5, 0.1875, ((0, 64),)),
        "coarse_channel_gain": draw_coarse_channel_gain(jax.random.fold_in(streams_of[4], 71), 0),
    }


def conv_taps(padded, kernel):
    rows = padded.shape[0] - 2
    cols = padded.shape[1]
    wide = jnp.pad(padded, ((0, 0), (1, 1), (0, 0)))
    parts = [wide[a:a + rows, b:b + cols, :] for a in range(3) for b in range(3)]
    stacked = jnp.concatenate(parts, axis=-1).reshape(rows * cols, -1)
    flat = kernel.reshape(-1, kernel.shape[-1])
    return jnp.dot(stacked, flat, preferred_element_type=jnp.float32).reshape(rows, cols, -1)


def layer_step(state, first, second_half):
    inner = jnp.pad(state.astype(jnp.bfloat16), ((1, 1), (0, 0), (0, 0)))
    hidden = jnp.tanh(conv_taps(inner, first)).astype(jnp.bfloat16)
    outer = conv_taps(jnp.pad(hidden, ((1, 1), (0, 0), (0, 0))), second_half)
    return state + 0.5 * jnp.tanh(outer)


def propagate(start, firsts, seconds):
    state = start
    for index in range(CF):
        state = layer_step(state, firsts[index], seconds[index])
    return state


def reference(coarse_states, first_kernels, second_kernels, coarse_channel_gain):
    firsts = first_kernels.reshape(COARSE_POINTS, CF, 9, C, C)
    seconds = second_kernels.reshape(COARSE_POINTS, CF, 9, C, C)

    def sweep_all(starts):
        return lax.map(lambda args: propagate(args[0], args[1], args[2]), (starts, firsts, seconds))

    y_first = sweep_all(coarse_states)
    c_first = jnp.concatenate([coarse_states[:1], y_first[:-1]], axis=0)
    y_second = sweep_all(c_first)
    resid = jnp.concatenate([jnp.zeros_like(c_first[:1]), y_second[:-1] - c_first[1:]], axis=0)

    def chain(carry, pair):
        gain, term = pair
        nxt = gain * carry + term
        return nxt, nxt

    zero_state = jnp.zeros(coarse_states.shape[1:], jnp.float32)
    _, errors = lax.scan(chain, zero_state, (coarse_channel_gain, resid))
    c_second = c_first + errors

    def points(args):
        state, fk, sk = args
        listing = [state]
        for index in range(CF - 1):
            state = layer_step(state, fk[index], sk[index])
            listing.append(state)
        return jnp.stack(listing, axis=0)

    result = lax.map(points, (c_second, firsts, seconds))
    return result.reshape(LAYERS, H, W, C), y_second
```

```python
import functools

import jax
import jax.numpy as jnp
from jax import lax
from jax.experimental import pallas as pl
from jax.experimental.pallas import tpu as pltpu
from jax.sharding import PartitionSpec as P

GROUP = 4
W = 128
C = 128


def widen_taps(taps, wide, slot):
    wide[slot, pl.ds(0, 9 * C), pl.ds(0, C)] = taps
    wide[slot, pl.ds(3 * C, 9 * C), pl.ds(C, C)] = taps


def spread(dst, pair, half, row):
    column = lax.broadcasted_iota(jnp.int32, (W, C), 0)
    before = jnp.where(column == 0, 0.0, pltpu.roll(row, 1, 0))
    after = jnp.where(column == W - 1, 0.0, pltpu.roll(row, W - 1, 0))
    for tap, part in enumerate((before, row, after)):
        dst[pair, :, pl.ds((half * 3 + tap) * C, C)] = part.astype(jnp.bfloat16)


def conv_pairs(src, wide, slot, pairs, emit):
    for first in range(0, pairs, GROUP):
        count = min(GROUP, pairs - first)
        low = src[pl.ds(first, count)].reshape(count * W, 6 * C)
        high = src[pl.ds(first + 1, count)].reshape(count * W, 6 * C)
        total = jnp.dot(
            low, wide[slot, pl.ds(0, 6 * C), :], preferred_element_type=jnp.float32
        ) + jnp.dot(high, wide[slot, pl.ds(6 * C, 6 * C), :], preferred_element_type=jnp.float32)
        for index in range(count):
            for half in range(2):
                emit(
                    first + index,
                    half,
                    total[index * W : (index + 1) * W, half * C : (half + 1) * C],
                )


def layers(count, halo, own, flags, state, fields, wide, firsts, seconds, after_layer):
    def keep(row, value):
        if row < halo:
            return value * flags[0]
        if row >= halo + own:
            return value * flags[1]
        return value

    rows = own + 2 * halo
    wide[:, pl.ds(9 * C, 3 * C), pl.ds(0, C)] = jnp.zeros((2, 3 * C, C), jnp.bfloat16)
    wide[:, pl.ds(0, 3 * C), pl.ds(C, C)] = jnp.zeros((2, 3 * C, C), jnp.bfloat16)
    for layer in range(count):
        widen_taps(firsts[layer], wide, 0)
        offset = 2 * layer + 1

        def hidden(pair, half, value, offset=offset):
            row = offset + 2 * pair + half
            spread(fields[1], pair, half, keep(row, jnp.tanh(value)))

        conv_pairs(fields[0], wide, 0, (rows - 2 * offset) // 2, hidden)
        widen_taps(seconds[layer], wide, 1)
        offset = 2 * layer + 2

        def outer(pair, half, value, offset=offset, last=layer == count - 1):
            row = offset + 2 * pair + half
            new = state[row] + 0.5 * keep(row, jnp.tanh(value))
            if not last:
                state[row] = new
                spread(fields[0], pair, half, new)
            after_layer(offset // 2, row, new)

        conv_pairs(fields[1], wide, 1, (rows - 2 * offset) // 2, outer)


def first_kernel(flags_ref, own_ref, top_ref, bottom_ref, firsts, seconds, y_ref, state, fa, fb, wide):
    own = own_ref.shape[0]
    halo = top_ref.shape[0]
    for row in range(own + 2 * halo):
        if row < halo:
            value = top_ref[row].astype(jnp.float32)
        elif row < halo + own:
            value = own_ref[row - halo]
        else:
            value = bottom_ref[row - halo - own].astype(jnp.float32)
        state[row] = value
        spread(fa, row // 2, row % 2, value)

    def after_layer(done, row, new):
        if done == firsts.shape[0]:
            y_ref[row - halo] = new.astype(jnp.bfloat16)

    flags = (flags_ref[0], flags_ref[1])
    layers(firsts.shape[0], halo, own, flags, state, (fa, fb), wide, firsts, seconds, after_layer)


def second_kernel(
    flags_ref, own_ref, top_ref, bottom_ref, got_ref, got_top_ref, got_bottom_ref, y_ref,
    firsts, seconds, relaxed_ref, resid_ref, state, fa, fb, wide,
):
    own = own_ref.shape[0]
    halo = top_ref.shape[0]
    start = flags_ref[2] > 0.5
    for row in range(own + 2 * halo):
        if row < halo:
            value = jnp.where(start, top_ref[row], got_top_ref[row]).astype(jnp.float32)
        elif row < halo + own:
            at = row - halo
            value = jnp.where(start, own_ref[at], got_ref[at].astype(jnp.float32))
        else:
            at = row - halo - own
            value = jnp.where(start, bottom_ref[at], got_bottom_ref[at]).astype(jnp.float32)
        state[row] = value
        spread(fa, row // 2, row % 2, value)

    def after_layer(done, row, new):
        if done == firsts.shape[0]:
            at = row - halo
            relaxed_ref[at] = new
            resid_ref[at] = (new - y_ref[at].astype(jnp.float32)).astype(jnp.bfloat16)

    flags = (flags_ref[0], flags_ref[1])
    layers(firsts.shape[0], halo, own, flags, state, (fa, fb), wide, firsts, seconds, after_layer)


def third_kernel(
    flags_ref, own_ref, top_ref, bottom_ref, got_ref, got_top_ref, got_bottom_ref,
    error_ref, error_top_ref, error_bottom_ref, firsts, seconds, states_ref, state, fa, fb, wide,
):
    own = own_ref.shape[0]
    halo = error_top_ref.shape[0]
    skip = top_ref.shape[0] - halo
    start = flags_ref[2] > 0.5
    for row in range(own + 2 * halo):
        if row < halo:
            value = jnp.where(start, top_ref[row + skip], got_top_ref[row + skip]).astype(jnp.float32)
            value = value + error_top_ref[row].astype(jnp.float32)
        elif row < halo + own:
            at = row - halo
            value = jnp.where(start, own_ref[at], got_ref[at].astype(jnp.float32))
            value = value + error_ref[at].astype(jnp.float32)
            states_ref[0, at] = value
        else:
            at = row - halo - own
            value = jnp.where(start, bottom_ref[at], got_bottom_ref[at]).astype(jnp.float32)
            value = value + error_bottom_ref[at].astype(jnp.float32)
        state[row] = value
        spread(fa, row // 2, row % 2, value)

    def after_layer(done, row, new):
        if halo <= row < halo + own:
            states_ref[done, row - halo] = new

    flags = (flags_ref[0], flags_ref[1])
    count = firsts.shape[0] - 1
    layers(count, halo, own, flags, state, (fa, fb), wide, firsts, seconds, after_layer)


def scan_kernel(gain_ref, resid_ref, error_ref):
    count = error_ref.shape[0]
    error_ref[0] = jnp.zeros(error_ref.shape[1:], error_ref.dtype)
    carry = jnp.zeros(error_ref.shape[1:], jnp.float32)
    for j in range(1, count):
        carry = gain_ref[pl.ds(j, 1), :] * carry + resid_ref[j - 1].astype(jnp.float32)
        error_ref[j] = carry.astype(error_ref.dtype)


def call(kernel, halo, own, outs, args):
    rows = own + 2 * halo
    in_specs = [pl.BlockSpec(memory_space=pltpu.SMEM)]
    in_specs += [pl.BlockSpec(memory_space=pltpu.VMEM)] * (len(args) - 1)
    return pl.pallas_call(
        kernel,
        out_shape=outs,
        in_specs=in_specs,
        out_specs=jax.tree.map(lambda _: pl.BlockSpec(memory_space=pltpu.VMEM), outs),
        scratch_shapes=[
            pltpu.VMEM((rows, W, C), jnp.float32),
            pltpu.VMEM((rows // 2, W, 6 * C), jnp.bfloat16),
            pltpu.VMEM((rows // 2, W, 6 * C), jnp.bfloat16),
            pltpu.VMEM((2, 12 * C, 2 * C), jnp.bfloat16),
        ],
        compiler_params=pltpu.CompilerParams(vmem_limit_bytes=40 * 2**20),
    )(*args)


def neighbour(block, up):
    count = lax.axis_size("space")
    route = [(i, i + 1) if up else (i + 1, i) for i in range(count - 1)]
    return lax.ppermute(block, "space", route)


def from_previous(block, shift):
    depth, space = lax.axis_size("depth"), lax.axis_size("space")
    route = [
        (d * space + s + shift, (d + 1) * space + s)
        for d in range(depth - 1)
        for s in range(space)
        if 0 <= s + shift < space
    ]
    return lax.ppermute(block, ("depth", "space"), route)


def shards(coarse_states, first_kernels, second_kernels, coarse_channel_gain):
    own_rows = coarse_states.shape[1]
    here = first_kernels.shape[0]
    bf16 = jnp.bfloat16
    start = coarse_states[0]
    depth = lax.axis_size("depth")
    slab = lax.axis_index("space")
    flags = jnp.stack(
        [slab > 0, slab < lax.axis_size("space") - 1, lax.axis_index("depth") == 0]
    ).astype(jnp.float32)
    firsts = first_kernels.reshape(here, 9 * C, C)
    seconds = second_kernels.reshape(here, 9 * C, C)

    halo = 2 * here
    rounded = start.astype(bf16)
    top = neighbour(rounded[own_rows - halo :], True)
    bottom = neighbour(rounded[:halo], False)
    field = jax.ShapeDtypeStruct(start.shape, bf16)
    y_first = call(
        first_kernel, halo, own_rows, field, (flags, start, top, bottom, firsts, seconds)
    )
    got_top = from_previous(y_first[own_rows - halo :], -1)
    got = from_previous(y_first, 0)
    got_bottom = from_previous(y_first[:halo], 1)
    relaxed, resid = call(
        second_kernel, halo, own_rows,
        (jax.ShapeDtypeStruct(start.shape, jnp.float32), field),
        (flags, start, top, bottom, got, got_top, got_bottom, y_first, firsts, seconds),
    )
    pixels = own_rows * W // depth
    columns = lax.all_to_all(resid.reshape(depth, pixels, C), "depth", 0, 0)
    errors = pl.pallas_call(
        scan_kernel, out_shape=jax.ShapeDtypeStruct(columns.shape, bf16)
    )(coarse_channel_gain, columns)
    error = lax.all_to_all(errors, "depth", 0, 0).reshape(start.shape)
    near = halo - 2
    error_top = neighbour(error[own_rows - near :], True)
    error_bottom = neighbour(error[:near], False)
    states = call(
        third_kernel, near, own_rows,
        jax.ShapeDtypeStruct((here,) + start.shape, jnp.float32),
        (flags, start, top, bottom, got, got_top, got_bottom, error, error_top, error_bottom,
         firsts, seconds),
    )
    return states, relaxed[None]


def solution(mesh):
    placed = (
        P("depth", "space", None, None),
        P("depth", None, None, None),
        P("depth", None, None, None),
        P(),
    )
    return jax.shard_map(
        shards,
        mesh=mesh,
        in_specs=placed,
        out_specs=(P("depth", "space", None, None), P("depth", "space", None, None)),
        check_vma=False,
    )
```

```python
import functools

import jax
import jax.numpy as jnp
from jax import lax
from jax.experimental import pallas as pl
from jax.experimental.pallas import tpu as pltpu
from jax.sharding import PartitionSpec as P

GROUP = 1
W = 128
C = 128
VMEM_LIMIT = 32 * 2**20
CODE_SCALE = 86.0 / 18.0


def round_kernel(start_ref, rounded_ref, own_ref, sems):
    copies = [
        pltpu.make_async_copy(start_ref.at[row], own_ref.at[row], sems.at[row])
        for row in range(own_ref.shape[0])
    ]
    for copy in copies:
        copy.start()
    for row, copy in enumerate(copies):
        copy.wait()
        rounded_ref[row] = own_ref[row].astype(jnp.bfloat16)


def taps_kernel(firsts, seconds, wide, sems):
    copies = []
    for at in range(wide.shape[0]):
        source = (firsts, seconds)[at % 2].at[at // 2]
        for half in range(2):
            copies.append(
                pltpu.make_async_copy(
                    source,
                    wide.at[at, pl.ds(half * 3 * C, 9 * C), pl.ds(half * C, C)],
                    sems.at[at, half],
                )
            )
    for copy in copies:
        copy.start()
    blank = jnp.zeros((3 * C, C), jnp.bfloat16)
    for at in range(wide.shape[0]):
        wide[at, pl.ds(9 * C, 3 * C), pl.ds(0, C)] = blank
        wide[at, pl.ds(0, 3 * C), pl.ds(C, C)] = blank
    for copy in copies:
        copy.wait()


def spread(dst, pair, half, row):
    column = lax.broadcasted_iota(jnp.int32, (W, C), 0)
    before = jnp.where(column == 0, 0.0, pltpu.roll(row, 1, 0))
    after = jnp.where(column == W - 1, 0.0, pltpu.roll(row, W - 1, 0))
    for tap, part in enumerate((before, row, after)):
        dst[pair, :, pl.ds((half * 3 + tap) * C, C)] = part.astype(jnp.bfloat16)


def conv_pairs(src, wide, slot, pairs, emit):
    for first in range(0, pairs, GROUP):
        count = min(GROUP, pairs - first)
        low = src[pl.ds(first, count)].reshape(count * W, 6 * C)
        high = src[pl.ds(first + 1, count)].reshape(count * W, 6 * C)
        total = jnp.dot(
            low, wide[slot, pl.ds(0, 6 * C), :], preferred_element_type=jnp.float32
        ) + jnp.dot(high, wide[slot, pl.ds(6 * C, 6 * C), :], preferred_element_type=jnp.float32)
        for index in range(count):
            for half in range(2):
                emit(
                    first + index,
                    half,
                    total[index * W : (index + 1) * W, half * C : (half + 1) * C],
                )


def layers(count, halo, own, state, fields, wide, after_layer):
    slab = lax.axis_index("space")
    above = (slab > 0).astype(jnp.float32)
    below = (slab < lax.axis_size("space") - 1).astype(jnp.float32)

    def keep(row, value):
        if row < halo:
            return value * above
        if row >= halo + own:
            return value * below
        return value

    rows = own + 2 * halo
    for layer in range(count):
        offset = 2 * layer + 1

        def hidden(pair, half, value, offset=offset):
            row = offset + 2 * pair + half
            spread(fields[1], pair, half, keep(row, jnp.tanh(value)))

        conv_pairs(fields[0], wide, 2 * layer, (rows - 2 * offset) // 2, hidden)
        offset = 2 * layer + 2

        def outer(pair, half, value, offset=offset, last=layer == count - 1):
            row = offset + 2 * pair + half
            new = state[row] + 0.5 * keep(row, jnp.tanh(value))
            if not last:
                state[row] = new
                spread(fields[0], pair, half, new)
            if halo <= row < halo + own:
                after_layer(offset // 2, row - halo, new)

        conv_pairs(fields[1], wide, 2 * layer + 1, (rows - 2 * offset) // 2, outer)


def load_rows(halo, own, value_of, state, field):
    for row in range(own + 2 * halo):
        value = value_of(row)
        state[row] = value
        spread(field, row // 2, row % 2, value)


def first_kernel(own_ref, wide, top_ref, bottom_ref, y_ref, state, fa, fb):
    own = own_ref.shape[0]
    halo = top_ref.shape[0]

    def value_of(row):
        if row < halo:
            return top_ref[row].astype(jnp.float32)
        if row >= halo + own:
            return bottom_ref[row - halo - own].astype(jnp.float32)
        return own_ref[row - halo]

    load_rows(halo, own, value_of, state, fa)

    def after_layer(done, row, new):
        if 2 * done == halo:
            y_ref[row] = new.astype(jnp.bfloat16)

    layers(halo // 2, halo, own, state, (fa, fb), wide, after_layer)


def second_kernel(own_ref, wide, top_ref, bottom_ref, got_ref, got_top_ref, got_bottom_ref, y_ref,
                  relaxed_ref, code_ref, state, fa, fb, kept, out_sems):
    own = own_ref.shape[0]
    halo = top_ref.shape[0]
    begin = lax.axis_index("depth") == 0

    def value_of(row):
        if row < halo:
            return jnp.where(begin, top_ref[row], got_top_ref[row]).astype(jnp.float32)
        if row >= halo + own:
            at = row - halo - own
            return jnp.where(begin, bottom_ref[at], got_bottom_ref[at]).astype(jnp.float32)
        return jnp.where(begin, own_ref[row - halo], got_ref[row - halo].astype(jnp.float32))

    load_rows(halo, own, value_of, state, fa)
    outs = []

    def after_layer(done, row, new):
        if 2 * done == halo:
            kept[row] = new
            outs.append(pltpu.make_async_copy(kept.at[row], relaxed_ref.at[row], out_sems.at[row]))
            outs[-1].start()
            resid = new - y_ref[row].astype(jnp.float32)
            code_ref[row] = jnp.exp(resid * CODE_SCALE).astype(jnp.bfloat16)

    layers(halo // 2, halo, own, state, (fa, fb), wide, after_layer)
    for out in outs:
        out.wait()


def third_kernel(own_ref, wide, top_ref, bottom_ref, got_ref, got_top_ref, got_bottom_ref,
                 error_ref, error_top_ref, error_bottom_ref, states_ref,
                 state, fa, fb, kept, out_sems):
    own = own_ref.shape[0]
    halo = error_top_ref.shape[0]
    skip = top_ref.shape[0] - halo
    begin = lax.axis_index("depth") == 0
    outs = []

    def put(done, row, value):
        kept[done, row] = value
        outs.append(
            pltpu.make_async_copy(
                kept.at[done, row], states_ref.at[done, row], out_sems.at[done, row]
            )
        )
        outs[-1].start()

    def value_of(row):
        if row < halo:
            value = jnp.where(begin, top_ref[row + skip], got_top_ref[row + skip])
            return value.astype(jnp.float32) + error_top_ref[row].astype(jnp.float32)
        if row >= halo + own:
            at = row - halo - own
            value = jnp.where(begin, bottom_ref[at], got_bottom_ref[at])
            return value.astype(jnp.float32) + error_bottom_ref[at].astype(jnp.float32)
        at = row - halo
        value = jnp.where(begin, own_ref[at], got_ref[at].astype(jnp.float32))
        value = value + error_ref[at].astype(jnp.float32)
        put(0, at, value)
        return value

    load_rows(halo, own, value_of, state, fa)
    layers(halo // 2, halo, own, state, (fa, fb), wide, put)
    for out in outs:
        out.wait()


def scan_kernel(gain_ref, code_ref, error_ref):
    count = error_ref.shape[0]
    error_ref[0] = jnp.zeros(error_ref.shape[1:], error_ref.dtype)
    carry = jnp.zeros(error_ref.shape[1:], jnp.float32)
    for j in range(1, count):
        resid = jnp.log(code_ref[j - 1].astype(jnp.float32)) * (1 / CODE_SCALE)
        carry = gain_ref[pl.ds(j, 1), :] * carry + resid
        error_ref[j] = carry.astype(error_ref.dtype)


def on_chip(count):
    return [pl.BlockSpec(memory_space=pltpu.VMEM)] * count


def sweep(kernel, halo, own, outs, args, kept=None):
    rows = own + 2 * halo
    scratch = [
        pltpu.VMEM((rows, W, C), jnp.float32),
        pltpu.VMEM((rows // 2, W, 6 * C), jnp.bfloat16),
        pltpu.VMEM((rows // 2, W, 6 * C), jnp.bfloat16),
    ]
    out_specs = on_chip(len(outs))
    if kept is not None:
        scratch += [pltpu.VMEM(outs[0].shape, jnp.float32), pltpu.SemaphoreType.DMA(kept)]
        out_specs[0] = pl.BlockSpec(memory_space=pltpu.HBM)
    flops = 2 * 9 * C * C * W * sum(rows - 2 * k for k in range(1, halo + 1))
    return pl.pallas_call(
        kernel,
        out_shape=outs,
        in_specs=on_chip(len(args)),
        out_specs=tuple(out_specs),
        scratch_shapes=scratch,
        compiler_params=pltpu.CompilerParams(vmem_limit_bytes=VMEM_LIMIT),
        cost_estimate=pl.CostEstimate(flops=flops, bytes_accessed=2**22, transcendentals=0),
    )(*args)


def neighbour(block, up):
    count = lax.axis_size("space")
    route = [(i, i + 1) if up else (i + 1, i) for i in range(count - 1)]
    return lax.ppermute(block, "space", route)


def from_previous(block, shift):
    depth, space = lax.axis_size("depth"), lax.axis_size("space")
    route = [
        (d * space + s + shift, (d + 1) * space + s)
        for d in range(depth - 1)
        for s in range(space)
        if 0 <= s + shift < space
    ]
    return lax.ppermute(block, ("depth", "space"), route)


def shards(coarse_states, first_kernels, second_kernels, coarse_channel_gain):
    here = first_kernels.shape[0]
    start = coarse_states[0]
    own = start.shape[0]
    depth = lax.axis_size("depth")
    wide_field = jax.ShapeDtypeStruct(start.shape, jnp.float32)
    field = jax.ShapeDtypeStruct(start.shape, jnp.bfloat16)
    hbm = pl.BlockSpec(memory_space=pltpu.HBM)

    halo = 2 * here
    rounded, start = pl.pallas_call(
        round_kernel,
        out_shape=(field, wide_field),
        in_specs=[hbm],
        out_specs=tuple(on_chip(2)),
        scratch_shapes=[pltpu.SemaphoreType.DMA((own,))],
        compiler_params=pltpu.CompilerParams(vmem_limit_bytes=VMEM_LIMIT),
    )(start)
    top = neighbour(rounded[own - halo :], True)
    bottom = neighbour(rounded[:halo], False)
    wide = pl.pallas_call(
        taps_kernel,
        out_shape=jax.ShapeDtypeStruct((2 * here, 12 * C, 2 * C), jnp.bfloat16),
        in_specs=[hbm, hbm],
        out_specs=pl.BlockSpec(memory_space=pltpu.VMEM),
        scratch_shapes=[pltpu.SemaphoreType.DMA((2 * here, 2))],
        compiler_params=pltpu.CompilerParams(vmem_limit_bytes=VMEM_LIMIT),
        cost_estimate=pl.CostEstimate(flops=0, bytes_accessed=2**24, transcendentals=0),
    )(first_kernels.reshape(here, 9 * C, C), second_kernels.reshape(here, 9 * C, C))

    (y_first,) = sweep(first_kernel, halo, own, (field,), (start, wide, top, bottom))
    got_top = from_previous(y_first[own - halo :], -1)
    got = from_previous(y_first, 0)
    got_bottom = from_previous(y_first[:halo], 1)
    before = (start, wide, top, bottom, got, got_top, got_bottom)
    relaxed, code = sweep(
        second_kernel, halo, own, (wide_field, field), before + (y_first,), kept=(own,)
    )
    pixels = own * W // depth
    columns = lax.all_to_all(code.reshape(depth, pixels, C), "depth", 0, 0)
    errors = pl.pallas_call(
        scan_kernel,
        out_shape=jax.ShapeDtypeStruct(columns.shape, jnp.bfloat16),
        in_specs=on_chip(2),
        out_specs=on_chip(1)[0],
        compiler_params=pltpu.CompilerParams(vmem_limit_bytes=VMEM_LIMIT),
    )(coarse_channel_gain, columns)
    error = lax.all_to_all(errors, "depth", 0, 0).reshape(start.shape)
    near = halo - 2
    error_top = neighbour(error[own - near :], True)
    error_bottom = neighbour(error[:near], False)
    (states,) = sweep(
        third_kernel, near, own, (jax.ShapeDtypeStruct((here,) + start.shape, jnp.float32),),
        before + (error, error_top, error_bottom), kept=(here, own),
    )
    return states, relaxed[None]


def solution(mesh):
    placed = (
        P("depth", "space", None, None),
        P("depth", None, None, None),
        P("depth", None, None, None),
        P(),
    )
    return jax.shard_map(
        shards,
        mesh=mesh,
        in_specs=placed,
        out_specs=(P("depth", "space", None, None), P("depth", "space", None, None)),
        check_vma=False,
    )
```

```python
import functools

import jax
import jax.numpy as jnp
from jax import lax
from jax.experimental import pallas as pl
from jax.experimental.pallas import tpu as pltpu
from jax.sharding import PartitionSpec as P

GROUP = 1
W = 128
C = 128
VMEM_LIMIT = 32 * 2**20
RESID_SCALE = 86.0 / 18.0
JOINED_SCALE = 86.0 / 36.0


def encode(value, scale):
    return jnp.exp(value * scale).astype(jnp.bfloat16)


def decode(code, scale):
    return jnp.log(code.astype(jnp.float32)) * (1 / scale)


def taps_kernel(start_ref, firsts, seconds, own_ref, wide, sems, own_sem):
    copies = [pltpu.make_async_copy(start_ref, own_ref, own_sem)]
    for at in range(wide.shape[0]):
        source = (firsts, seconds)[at % 2].at[at // 2]
        for half in range(2):
            copies.append(
                pltpu.make_async_copy(
                    source,
                    wide.at[at, pl.ds(half * 3 * C, 9 * C), pl.ds(half * C, C)],
                    sems.at[at, half],
                )
            )
    for copy in copies:
        copy.start()
    blank = jnp.zeros((3 * C, C), jnp.bfloat16)
    for at in range(wide.shape[0]):
        wide[at, pl.ds(9 * C, 3 * C), pl.ds(0, C)] = blank
        wide[at, pl.ds(0, 3 * C), pl.ds(C, C)] = blank
    for copy in copies:
        copy.wait()


def spread(dst, pair, half, row):
    column = lax.broadcasted_iota(jnp.int32, (W, C), 0)
    before = jnp.where(column == 0, 0.0, pltpu.roll(row, 1, 0))
    after = jnp.where(column == W - 1, 0.0, pltpu.roll(row, W - 1, 0))
    for tap, part in enumerate((before, row, after)):
        dst[pair, :, pl.ds((half * 3 + tap) * C, C)] = part.astype(jnp.bfloat16)


def conv_pairs(src, wide, slot, pairs, emit):
    for first in range(0, pairs, GROUP):
        count = min(GROUP, pairs - first)
        low = src[pl.ds(first, count)].reshape(count * W, 6 * C)
        high = src[pl.ds(first + 1, count)].reshape(count * W, 6 * C)
        total = jnp.dot(
            low, wide[slot, pl.ds(0, 6 * C), :], preferred_element_type=jnp.float32
        ) + jnp.dot(high, wide[slot, pl.ds(6 * C, 6 * C), :], preferred_element_type=jnp.float32)
        for index in range(count):
            for half in range(2):
                emit(
                    first + index,
                    half,
                    total[index * W : (index + 1) * W, half * C : (half + 1) * C],
                )


def layers(count, halo, own, state, fields, wide, after_layer):
    slab = lax.axis_index("space")
    above = (slab > 0).astype(jnp.float32)
    below = (slab < lax.axis_size("space") - 1).astype(jnp.float32)

    def keep(row, value):
        if row < halo:
            return value * above
        if row >= halo + own:
            return value * below
        return value

    rows = own + 2 * halo
    for layer in range(count):
        offset = 2 * layer + 1

        def hidden(pair, half, value, offset=offset):
            row = offset + 2 * pair + half
            spread(fields[1], pair, half, keep(row, jnp.tanh(value)))

        conv_pairs(fields[0], wide, 2 * layer, (rows - 2 * offset) // 2, hidden)
        offset = 2 * layer + 2

        def outer(pair, half, value, offset=offset, last=layer == count - 1):
            row = offset + 2 * pair + half
            new = state[row] + 0.5 * keep(row, jnp.tanh(value))
            if not last:
                state[row] = new
                spread(fields[0], pair, half, new)
            if halo <= row < halo + own:
                after_layer(offset // 2, row - halo, new)

        conv_pairs(fields[1], wide, 2 * layer + 1, (rows - 2 * offset) // 2, outer)


def load_rows(halo, own, value_of, state, field):
    for row in range(own + 2 * halo):
        value = value_of(row)
        state[row] = value
        spread(field, row // 2, row % 2, value)


def first_kernel(own_ref, wide, top_ref, bottom_ref, y_ref, state, fa, fb):
    own = own_ref.shape[0]
    halo = top_ref.shape[0]

    def value_of(row):
        if row < halo:
            return top_ref[row].astype(jnp.float32)
        if row >= halo + own:
            return bottom_ref[row - halo - own].astype(jnp.float32)
        return own_ref[row - halo]

    load_rows(halo, own, value_of, state, fa)

    def after_layer(done, row, new):
        if 2 * done == halo:
            y_ref[row] = new.astype(jnp.bfloat16)

    layers(halo // 2, halo, own, state, (fa, fb), wide, after_layer)


def second_kernel(own_ref, wide, top_ref, bottom_ref, got_ref, got_top_ref, got_bottom_ref, y_ref,
                  relaxed_ref, code_ref, state, fa, fb):
    own = own_ref.shape[0]
    halo = top_ref.shape[0]
    begin = lax.axis_index("depth") == 0

    def value_of(row):
        if row < halo:
            return jnp.where(begin, top_ref[row], got_top_ref[row]).astype(jnp.float32)
        if row >= halo + own:
            at = row - halo - own
            return jnp.where(begin, bottom_ref[at], got_bottom_ref[at]).astype(jnp.float32)
        return jnp.where(begin, own_ref[row - halo], got_ref[row - halo].astype(jnp.float32))

    load_rows(halo, own, value_of, state, fa)

    def after_layer(done, row, new):
        if 2 * done == halo:
            relaxed_ref[row] = new
            resid = new - y_ref[row].astype(jnp.float32)
            code_ref[row] = encode(resid, RESID_SCALE)

    layers(halo // 2, halo, own, state, (fa, fb), wide, after_layer)


def third_kernel(own_ref, wide, top_ref, bottom_ref, got_ref, got_top_ref, got_bottom_ref,
                 error_ref, error_top_ref, error_bottom_ref, y_ref, states_ref, relaxed_ref,
                 state, fa, fb, kept, out_sems, relaxed_sem):
    own = own_ref.shape[0]
    halo = error_top_ref.shape[0]
    skip = top_ref.shape[0] - halo
    begin = lax.axis_index("depth") == 0
    outs = [pltpu.make_async_copy(y_ref, relaxed_ref, relaxed_sem)]
    outs[0].start()

    def put(done, row, value):
        kept[done, row] = value
        outs.append(
            pltpu.make_async_copy(
                kept.at[done, row], states_ref.at[done, row], out_sems.at[done, row]
            )
        )
        outs[-1].start()

    def value_of(row):
        if row < halo:
            value = jnp.where(begin, top_ref[row + skip], got_top_ref[row + skip])
            return value.astype(jnp.float32) + error_top_ref[row].astype(jnp.float32)
        if row >= halo + own:
            at = row - halo - own
            value = jnp.where(begin, bottom_ref[at], got_bottom_ref[at])
            return value.astype(jnp.float32) + error_bottom_ref[at].astype(jnp.float32)
        at = row - halo
        value = jnp.where(begin, own_ref[at], got_ref[at].astype(jnp.float32))
        value = value + error_ref[at].astype(jnp.float32)
        put(0, at, value)
        return value

    load_rows(halo, own, value_of, state, fa)
    layers(halo // 2, halo, own, state, (fa, fb), wide, put)
    for out in outs:
        out.wait()


def join_kernel(gain_ref, codes_ref, joined_ref):
    depth = lax.axis_index("depth")
    rows = joined_ref.shape[0]
    first = lax.rem(depth, 2) * rows
    later = lax.min(depth - lax.rem(depth, 2) + 2, gain_ref.shape[0] - 1)
    gain = gain_ref[pl.ds(later, 1), :]
    for row in range(rows):
        early = decode(codes_ref[0, first + row], RESID_SCALE)
        late = decode(codes_ref[1, first + row], RESID_SCALE)
        joined_ref[row] = encode(gain * early + late, JOINED_SCALE)


def scan_kernel(gain_ref, joined_ref, error_ref):
    count = error_ref.shape[0]
    carry = jnp.zeros(error_ref.shape[1:], jnp.float32)
    error_ref[0] = carry.astype(error_ref.dtype)
    for k in range(count - 1):
        gain = gain_ref[pl.ds(2 * k + 1, 1), :] * gain_ref[pl.ds(2 * k + 2, 1), :]
        carry = gain * carry + decode(joined_ref[k], JOINED_SCALE)
        error_ref[k + 1] = carry.astype(error_ref.dtype)


def split_kernel(gain_ref, codes_ref, pair_ref, error_ref, upper_ref, lower_ref):
    depth = lax.axis_index("depth")
    rows = error_ref.shape[0]
    near = upper_ref.shape[0]
    odd = lax.rem(depth, 2) == 1
    gain = gain_ref[pl.ds(depth, 1), :]
    for row in range(rows):
        error = pair_ref[row].astype(jnp.float32)
        own = gain * error + decode(codes_ref[0, row], RESID_SCALE)
        value = jnp.where(odd, own, error).astype(jnp.bfloat16)
        error_ref[row] = value
        if row < near:
            upper_ref[row] = value
        if row >= rows - near:
            lower_ref[row - rows + near] = value


def on_chip(count):
    return [pl.BlockSpec(memory_space=pltpu.VMEM)] * count


def small(kernel, outs, *args):
    return pl.pallas_call(
        kernel,
        out_shape=outs,
        in_specs=on_chip(len(args)),
        out_specs=jax.tree.map(lambda _: on_chip(1)[0], outs),
        compiler_params=pltpu.CompilerParams(vmem_limit_bytes=VMEM_LIMIT),
    )(*args)


def sweep(kernel, halo, own, outs, args, kept=None):
    rows = own + 2 * halo
    scratch = [
        pltpu.VMEM((rows, W, C), jnp.float32),
        pltpu.VMEM((rows // 2, W, 6 * C), jnp.bfloat16),
        pltpu.VMEM((rows // 2, W, 6 * C), jnp.bfloat16),
    ]
    out_specs = on_chip(len(outs))
    if kept is not None:
        scratch += [
            pltpu.VMEM(outs[0].shape, jnp.float32),
            pltpu.SemaphoreType.DMA(kept),
            pltpu.SemaphoreType.DMA,
        ]
        out_specs = [pl.BlockSpec(memory_space=pltpu.HBM)] * len(outs)
    flops = 2 * 9 * C * C * W * sum(rows - 2 * k for k in range(1, halo + 1))
    return pl.pallas_call(
        kernel,
        out_shape=outs,
        in_specs=on_chip(len(args)),
        out_specs=tuple(out_specs),
        scratch_shapes=scratch,
        compiler_params=pltpu.CompilerParams(vmem_limit_bytes=VMEM_LIMIT),
        cost_estimate=pl.CostEstimate(flops=flops, bytes_accessed=2**22, transcendentals=0),
    )(*args)


def neighbour(block, up):
    count = lax.axis_size("space")
    route = [(i, i + 1) if up else (i + 1, i) for i in range(count - 1)]
    return lax.ppermute(block, "space", route)


def from_previous(block, shift):
    depth, space = lax.axis_size("depth"), lax.axis_size("space")
    route = [
        (d * space + s + shift, (d + 1) * space + s)
        for d in range(depth - 1)
        for s in range(space)
        if 0 <= s + shift < space
    ]
    return lax.ppermute(block, ("depth", "space"), route)


def shards(coarse_states, first_kernels, second_kernels, coarse_channel_gain):
    here = first_kernels.shape[0]
    start = coarse_states[0]
    own = start.shape[0]
    depth = lax.axis_size("depth")
    wide_field = jax.ShapeDtypeStruct(start.shape, jnp.float32)
    field = jax.ShapeDtypeStruct(start.shape, jnp.bfloat16)
    hbm = pl.BlockSpec(memory_space=pltpu.HBM)

    halo = 2 * here
    rounded = start.astype(jnp.bfloat16)
    top = neighbour(rounded[own - halo :], True)
    bottom = neighbour(rounded[:halo], False)
    start, wide = pl.pallas_call(
        taps_kernel,
        out_shape=(
            wide_field,
            jax.ShapeDtypeStruct((2 * here, 12 * C, 2 * C), jnp.bfloat16),
        ),
        in_specs=[hbm, hbm, hbm],
        out_specs=tuple(on_chip(2)),
        scratch_shapes=[pltpu.SemaphoreType.DMA((2 * here, 2)), pltpu.SemaphoreType.DMA],
        compiler_params=pltpu.CompilerParams(vmem_limit_bytes=VMEM_LIMIT),
        cost_estimate=pl.CostEstimate(flops=0, bytes_accessed=2**24, transcendentals=0),
    )(start, first_kernels.reshape(here, 9 * C, C), second_kernels.reshape(here, 9 * C, C))

    (y_first,) = sweep(first_kernel, halo, own, (field,), (start, wide, top, bottom))
    got_top = from_previous(y_first[own - halo :], -1)
    got = from_previous(y_first, 0)
    got_bottom = from_previous(y_first[:halo], 1)
    before = (start, wide, top, bottom, got, got_top, got_bottom)
    y_second, code = sweep(
        second_kernel, halo, own, (wide_field, field), before + (y_first,)
    )
    pairs = [[at, at + 1] for at in range(0, depth, 2)]
    alike = [list(range(core, depth, 2)) for core in range(2)]
    codes = lax.all_gather(code, "depth", axis_index_groups=pairs)
    half = jax.ShapeDtypeStruct((own // 2,) + field.shape[1:], jnp.bfloat16)
    joined = small(join_kernel, half, coarse_channel_gain, codes)
    joined = joined.reshape(depth // 2, own * W // depth, C)
    joined = lax.all_to_all(joined, "depth", 0, 0, axis_index_groups=alike)
    errors = small(
        scan_kernel, jax.ShapeDtypeStruct(joined.shape, jnp.bfloat16), coarse_channel_gain, joined
    )
    errors = lax.all_to_all(errors, "depth", 0, 0, axis_index_groups=alike)
    pair = lax.all_gather(errors.reshape(half.shape), "depth", axis_index_groups=pairs)
    near = halo - 2
    part = jax.ShapeDtypeStruct((near,) + field.shape[1:], jnp.bfloat16)
    error, upper, lower = small(
        split_kernel, (field, part, part), coarse_channel_gain, codes, pair.reshape(field.shape)
    )
    error_top = neighbour(lower, True)
    error_bottom = neighbour(upper, False)
    states, relaxed = sweep(
        third_kernel, near, own,
        (jax.ShapeDtypeStruct((here,) + start.shape, jnp.float32), wide_field),
        before + (error, error_top, error_bottom, y_second), kept=(here, own),
    )
    return states, relaxed[None]


def solution(mesh):
    placed = (
        P("depth", "space", None, None),
        P("depth", None, None, None),
        P("depth", None, None, None),
        P(),
    )
    return jax.shard_map(
        shards,
        mesh=mesh,
        in_specs=placed,
        out_specs=(P("depth", "space", None, None), P("depth", "space", None, None)),
        check_vma=False,
    )
```

```python
import functools

import jax
import jax.numpy as jnp
from jax import lax
from jax.experimental import pallas as pl
from jax.experimental.pallas import tpu as pltpu
from jax.sharding import PartitionSpec as P

W = 128
C = 128
VMEM_LIMIT = 32 * 2**20
RESID_SCALE = 86.0 / 18.0
JOINED_SCALE = 86.0 / 36.0


def encode(value, scale):
    return jnp.exp(value * scale).astype(jnp.bfloat16)


def decode(code, scale):
    return jnp.log(code.astype(jnp.float32)) * (1 / scale)


def taps_kernel(start_ref, firsts, seconds, own_ref, wide, sems, own_sem):
    copies = [pltpu.make_async_copy(start_ref, own_ref, own_sem)]
    for at in range(wide.shape[0]):
        source = (firsts, seconds)[at % 2].at[at // 2]
        for half in range(2):
            copies.append(
                pltpu.make_async_copy(
                    source,
                    wide.at[at, pl.ds(half * 3 * C, 9 * C), pl.ds(half * C, C)],
                    sems.at[at, half],
                )
            )
    for copy in copies:
        copy.start()
    blank = jnp.zeros((3 * C, C), jnp.bfloat16)
    for at in range(wide.shape[0]):
        wide[at, pl.ds(9 * C, 3 * C), pl.ds(0, C)] = blank
        wide[at, pl.ds(0, 3 * C), pl.ds(C, C)] = blank
    for copy in copies:
        copy.wait()


def spread(dst, pair, half, row):
    column = lax.broadcasted_iota(jnp.int32, (W, C), 0)
    before = jnp.where(column == 0, 0.0, pltpu.roll(row, 1, 0))
    after = jnp.where(column == W - 1, 0.0, pltpu.roll(row, W - 1, 0))
    for tap, part in enumerate((before, row, after)):
        dst[pair, :, pl.ds((half * 3 + tap) * C, C)] = part.astype(jnp.bfloat16)


def conv_pair(src, wide, slot, pair, emit):
    total = jnp.dot(
        src[pair], wide[slot, pl.ds(0, 6 * C), :], preferred_element_type=jnp.float32
    ) + jnp.dot(src[pair + 1], wide[slot, pl.ds(6 * C, 6 * C), :], preferred_element_type=jnp.float32)
    for half in range(2):
        emit(pair, half, total[:, half * C : (half + 1) * C])


def inner_steps(own, value_of, wide, mid, parts):
    values = {}
    for row in range(own):
        values[row] = value_of(row)
        spread(parts[0], row // 2, row % 2, values[row])
    for step in range(1, len(parts)):

        def hidden(pair, half, value, step=step):
            spread(parts[step], pair, half, jnp.tanh(value))

        def outer(pair, half, value, step=step):
            new = value_of(step + 2 * pair + half) + 0.5 * jnp.tanh(value)
            mid[2 * pair + half] = new
            spread(parts[step], pair, half, new)

        for pair in range(inner_pairs(own, step)):
            conv_pair(parts[step - 1], wide, step - 1, pair, outer if step % 2 == 0 else hidden)


def first_inner(own_ref, wide, mid, *parts):
    inner_steps(own_ref.shape[0], lambda row: own_ref[row], wide, mid, parts)


def third_inner(own_ref, wide, got_ref, error_ref, begin_ref, mid, *parts):
    begin = lax.axis_index("depth") == 0
    for row in range(own_ref.shape[0]):
        value = jnp.where(begin, own_ref[row], got_ref[row].astype(jnp.float32))
        begin_ref[row] = value + error_ref[row].astype(jnp.float32)
    inner_steps(own_ref.shape[0], lambda row: begin_ref[row], wide, mid, parts)


def layers(count, halo, own, state, fields, wide, after_layer, mid, parts):
    slab = lax.axis_index("space")
    above = (slab > 0).astype(jnp.float32)
    below = (slab < lax.axis_size("space") - 1).astype(jnp.float32)

    def keep(row, value):
        if row < halo:
            return value * above
        if row >= halo + own:
            return value * below
        return value

    rows = own + 2 * halo
    for step in range(1, 2 * count + 1):
        src, dst = fields[(step - 1) % 2], fields[step % 2]
        inside = range(halo // 2, halo // 2 + inner_pairs(own, step)) if parts else ()

        def hidden(pair, half, value, step=step, dst=dst):
            row = step + 2 * pair + half
            spread(dst, pair, half, keep(row, jnp.tanh(value)))

        def outer(pair, half, value, step=step, dst=dst):
            row = step + 2 * pair + half
            new = state[row] + 0.5 * keep(row, jnp.tanh(value))
            if step < 2 * count:
                state[row] = new
                spread(dst, pair, half, new)
            if halo <= row < halo + own:
                after_layer(step // 2, row - halo, new)

        for pair in range((rows - 2 * step) // 2):
            if pair not in inside:
                conv_pair(src, wide, step - 1, pair, outer if step % 2 == 0 else hidden)
                continue
            dst[pair] = parts[step][pair - halo // 2]
            if step % 2 == 0:
                for half in range(2):
                    row = step + 2 * pair + half
                    new = mid[2 * (pair - halo // 2) + half]
                    state[row] = new
                    after_layer(step // 2, row - halo, new)


def inner_pairs(own, step):
    return max(own // 2 - step, 0)


def load_rows(halo, own, value_of, state, field, part):
    for row in range(own + 2 * halo):
        value = value_of(row)
        state[row] = value
        if part is None or not halo <= row < halo + own:
            spread(field, row // 2, row % 2, value)
    if part is not None:
        for pair in range(own // 2):
            field[halo // 2 + pair] = part[pair]


def first_kernel(own_ref, wide, top_ref, bottom_ref, mid, *refs):
    parts, (y_ref, state, fa, fb) = refs[:-4], refs[-4:]
    own = own_ref.shape[0]
    halo = top_ref.shape[0]

    def value_of(row):
        if row < halo:
            return top_ref[row].astype(jnp.float32)
        if row >= halo + own:
            return bottom_ref[row - halo - own].astype(jnp.float32)
        return own_ref[row - halo]

    load_rows(halo, own, value_of, state, fa, parts[0])

    def after_layer(done, row, new):
        if 2 * done == halo:
            y_ref[row] = new.astype(jnp.bfloat16)

    layers(halo // 2, halo, own, state, (fa, fb), wide, after_layer, mid, parts)


def second_kernel(own_ref, wide, top_ref, bottom_ref, got_ref, got_top_ref, got_bottom_ref, y_ref,
                  relaxed_ref, code_ref, state, fa, fb):
    own = own_ref.shape[0]
    halo = top_ref.shape[0]
    begin = lax.axis_index("depth") == 0

    def value_of(row):
        if row < halo:
            return jnp.where(begin, top_ref[row], got_top_ref[row]).astype(jnp.float32)
        if row >= halo + own:
            at = row - halo - own
            return jnp.where(begin, bottom_ref[at], got_bottom_ref[at]).astype(jnp.float32)
        return jnp.where(begin, own_ref[row - halo], got_ref[row - halo].astype(jnp.float32))

    load_rows(halo, own, value_of, state, fa, None)

    def after_layer(done, row, new):
        if 2 * done == halo:
            relaxed_ref[row] = new
            resid = new - y_ref[row].astype(jnp.float32)
            code_ref[row] = encode(resid, RESID_SCALE)

    layers(halo // 2, halo, own, state, (fa, fb), wide, after_layer, None, ())


def third_kernel(own_ref, wide, top_ref, bottom_ref, got_top_ref, got_bottom_ref,
                 error_top_ref, error_bottom_ref, y_ref, mid, *refs):
    parts, (states_ref, relaxed_ref, state, fa, fb, kept, out_sems, relaxed_sem) = refs[:-8], refs[-8:]
    own = own_ref.shape[0]
    halo = error_top_ref.shape[0]
    skip = top_ref.shape[0] - halo
    begin = lax.axis_index("depth") == 0
    outs = [
        pltpu.make_async_copy(y_ref, relaxed_ref, relaxed_sem),
        pltpu.make_async_copy(own_ref, states_ref.at[0], out_sems.at[0, 0]),
    ]
    for out in outs:
        out.start()

    def put(done, row, value):
        kept[done, row] = value
        outs.append(
            pltpu.make_async_copy(
                kept.at[done, row], states_ref.at[done, row], out_sems.at[done, row]
            )
        )
        outs[-1].start()

    def value_of(row):
        if row < halo:
            value = jnp.where(begin, top_ref[row + skip], got_top_ref[row + skip])
            return value.astype(jnp.float32) + error_top_ref[row].astype(jnp.float32)
        if row >= halo + own:
            at = row - halo - own
            value = jnp.where(begin, bottom_ref[at], got_bottom_ref[at])
            return value.astype(jnp.float32) + error_bottom_ref[at].astype(jnp.float32)
        return own_ref[row - halo]

    load_rows(halo, own, value_of, state, fa, parts[0])
    layers(halo // 2, halo, own, state, (fa, fb), wide, put, mid, parts)
    for out in outs:
        out.wait()


def join_kernel(gain_ref, codes_ref, joined_ref):
    depth = lax.axis_index("depth")
    rows = joined_ref.shape[0]
    first = lax.rem(depth, 2) * rows
    later = lax.min(depth - lax.rem(depth, 2) + 2, gain_ref.shape[0] - 1)
    gain = gain_ref[pl.ds(later, 1), :]
    for row in range(rows):
        early = decode(codes_ref[0, first + row], RESID_SCALE)
        late = decode(codes_ref[1, first + row], RESID_SCALE)
        joined_ref[row] = encode(gain * early + late, JOINED_SCALE)


def scan_kernel(gain_ref, joined_ref, error_ref):
    count = error_ref.shape[0]
    carry = jnp.zeros(error_ref.shape[1:], jnp.float32)
    error_ref[0] = carry.astype(error_ref.dtype)
    for k in range(count - 1):
        gain = gain_ref[pl.ds(2 * k + 1, 1), :] * gain_ref[pl.ds(2 * k + 2, 1), :]
        carry = gain * carry + decode(joined_ref[k], JOINED_SCALE)
        error_ref[k + 1] = carry.astype(error_ref.dtype)


def split_kernel(gain_ref, codes_ref, pair_ref, error_ref, upper_ref, lower_ref):
    depth = lax.axis_index("depth")
    rows = error_ref.shape[0]
    near = upper_ref.shape[0]
    odd = lax.rem(depth, 2) == 1
    gain = gain_ref[pl.ds(depth, 1), :]
    for row in range(rows):
        error = pair_ref[row].astype(jnp.float32)
        own = gain * error + decode(codes_ref[0, row], RESID_SCALE)
        value = jnp.where(odd, own, error).astype(jnp.bfloat16)
        error_ref[row] = value
        if row < near:
            upper_ref[row] = value
        if row >= rows - near:
            lower_ref[row - rows + near] = value


def on_chip(count):
    return [pl.BlockSpec(memory_space=pltpu.VMEM)] * count


def small(kernel, outs, *args, flops=1):
    return pl.pallas_call(
        kernel,
        out_shape=outs,
        in_specs=on_chip(len(args)),
        out_specs=jax.tree.map(lambda _: on_chip(1)[0], outs),
        compiler_params=pltpu.CompilerParams(vmem_limit_bytes=VMEM_LIMIT),
        cost_estimate=pl.CostEstimate(
            flops=flops * 36 * C * C * W, bytes_accessed=2**19, transcendentals=0
        ),
    )(*args)


def sweep(kernel, halo, own, outs, args, kept=None):
    rows = own + 2 * halo
    scratch = [
        pltpu.VMEM((rows, W, C), jnp.float32),
        pltpu.VMEM((rows // 2, W, 6 * C), jnp.bfloat16),
        pltpu.VMEM((rows // 2, W, 6 * C), jnp.bfloat16),
    ]
    out_specs = on_chip(len(outs))
    if kept is not None:
        scratch += [
            pltpu.VMEM(outs[0].shape, jnp.float32),
            pltpu.SemaphoreType.DMA(kept),
            pltpu.SemaphoreType.DMA,
        ]
        out_specs = [pl.BlockSpec(memory_space=pltpu.HBM)] * len(outs)
    flops = 2 * 9 * C * C * W * sum(rows - 2 * k for k in range(1, halo + 1))
    return pl.pallas_call(
        kernel,
        out_shape=outs,
        in_specs=on_chip(len(args)),
        out_specs=tuple(out_specs),
        scratch_shapes=scratch,
        compiler_params=pltpu.CompilerParams(vmem_limit_bytes=VMEM_LIMIT),
        cost_estimate=pl.CostEstimate(flops=flops, bytes_accessed=2**22, transcendentals=0),
    )(*args)


def neighbour(block, up):
    count = lax.axis_size("space")
    route = [(i, i + 1) if up else (i + 1, i) for i in range(count - 1)]
    return lax.ppermute(block, "space", route)


def from_previous(block, shift):
    depth, space = lax.axis_size("depth"), lax.axis_size("space")
    route = [
        (d * space + s + shift, (d + 1) * space + s)
        for d in range(depth - 1)
        for s in range(space)
        if 0 <= s + shift < space
    ]
    return lax.ppermute(block, ("depth", "space"), route)


def shards(coarse_states, first_kernels, second_kernels, coarse_channel_gain):
    here = first_kernels.shape[0]
    start = coarse_states[0]
    own = start.shape[0]
    depth = lax.axis_size("depth")
    wide_field = jax.ShapeDtypeStruct(start.shape, jnp.float32)
    field = jax.ShapeDtypeStruct(start.shape, jnp.bfloat16)
    hbm = pl.BlockSpec(memory_space=pltpu.HBM)

    halo = 2 * here
    rounded = start.astype(jnp.bfloat16)
    top = neighbour(rounded[own - halo :], True)
    bottom = neighbour(rounded[:halo], False)
    start, wide = pl.pallas_call(
        taps_kernel,
        out_shape=(
            wide_field,
            jax.ShapeDtypeStruct((2 * here, 12 * C, 2 * C), jnp.bfloat16),
        ),
        in_specs=[hbm, hbm, hbm],
        out_specs=tuple(on_chip(2)),
        scratch_shapes=[pltpu.SemaphoreType.DMA((2 * here, 2)), pltpu.SemaphoreType.DMA],
        compiler_params=pltpu.CompilerParams(vmem_limit_bytes=VMEM_LIMIT),
        cost_estimate=pl.CostEstimate(flops=0, bytes_accessed=2**24, transcendentals=0),
    )(start, first_kernels.reshape(here, 9 * C, C), second_kernels.reshape(here, 9 * C, C))

    inner = [jax.ShapeDtypeStruct((own - 4,) + field.shape[1:], jnp.float32)] + [
        jax.ShapeDtypeStruct((inner_pairs(own, step), W, 6 * C), jnp.bfloat16)
        for step in range(own // 2)
    ]
    pairs_inside = sum(inner_pairs(own, step) for step in range(1, own // 2))
    known = small(first_inner, inner, start, wide, flops=pairs_inside)
    (y_first,) = sweep(first_kernel, halo, own, (field,), (start, wide, top, bottom, *known))
    got_top = from_previous(y_first[own - halo :], -1)
    got = from_previous(y_first, 0)
    got_bottom = from_previous(y_first[:halo], 1)
    before = (start, wide, top, bottom, got, got_top, got_bottom)
    y_second, code = sweep(
        second_kernel, halo, own, (wide_field, field), before + (y_first,)
    )
    pairs = [[at, at + 1] for at in range(0, depth, 2)]
    alike = [list(range(core, depth, 2)) for core in range(2)]
    codes = lax.all_gather(code, "depth", axis_index_groups=pairs)
    half = jax.ShapeDtypeStruct((own // 2,) + field.shape[1:], jnp.bfloat16)
    joined = small(join_kernel, half, coarse_channel_gain, codes)
    joined = joined.reshape(depth // 2, own * W // depth, C)
    joined = lax.all_to_all(joined, "depth", 0, 0, axis_index_groups=alike)
    errors = small(
        scan_kernel, jax.ShapeDtypeStruct(joined.shape, jnp.bfloat16), coarse_channel_gain, joined
    )
    errors = lax.all_to_all(errors, "depth", 0, 0, axis_index_groups=alike)
    pair = lax.all_gather(errors.reshape(half.shape), "depth", axis_index_groups=pairs)
    near = halo - 2
    part = jax.ShapeDtypeStruct((near,) + field.shape[1:], jnp.bfloat16)
    error, upper, lower = small(
        split_kernel, (field, part, part), coarse_channel_gain, codes, pair.reshape(field.shape)
    )
    error_top = neighbour(lower, True)
    error_bottom = neighbour(upper, False)
    begin, *known = small(
        third_inner, [wide_field] + inner, start, wide, got, error, flops=pairs_inside
    )
    states, relaxed = sweep(
        third_kernel, near, own,
        (jax.ShapeDtypeStruct((here,) + start.shape, jnp.float32), wide_field),
        (begin, wide, top, bottom, got_top, got_bottom, error_top, error_bottom, y_second, *known),
        kept=(here, own),
    )
    return states, relaxed[None]


def solution(mesh):
    placed = (
        P("depth", "space", None, None),
        P("depth", None, None, None),
        P("depth", None, None, None),
        P(),
    )
    return jax.shard_map(
        shards,
        mesh=mesh,
        in_specs=placed,
        out_specs=(P("depth", "space", None, None), P("depth", "space", None, None)),
        check_vma=False,
    )
```

```python
import functools

import jax
import jax.numpy as jnp
from jax import lax
from jax.experimental import pallas as pl
from jax.experimental.pallas import tpu as pltpu
from jax.sharding import PartitionSpec as P

W = 128
C = 128
VMEM_LIMIT = 32 * 2**20
RESID_SCALE = 86.0 / 18.0
JOINED_SCALE = 86.0 / 36.0


def encode(value, scale):
    return jnp.exp(value * scale).astype(jnp.bfloat16)


def decode(code, scale):
    return jnp.log(code.astype(jnp.float32)) * (1 / scale)


def taps_kernel(start_ref, firsts, seconds, own_ref, wide, sems, own_sem):
    copies = [pltpu.make_async_copy(start_ref, own_ref, own_sem)]
    for at in range(wide.shape[0]):
        source = (firsts, seconds)[at % 2].at[at // 2]
        for half in range(2):
            copies.append(
                pltpu.make_async_copy(
                    source,
                    wide.at[at, pl.ds(half * 3 * C, 9 * C), pl.ds(half * C, C)],
                    sems.at[at, half],
                )
            )
    for copy in copies:
        copy.start()
    blank = jnp.zeros((3 * C, C), jnp.bfloat16)
    for at in range(wide.shape[0]):
        wide[at, pl.ds(9 * C, 3 * C), pl.ds(0, C)] = blank
        wide[at, pl.ds(0, 3 * C), pl.ds(C, C)] = blank
    for copy in copies:
        copy.wait()


def spread(dst, pair, half, row):
    column = lax.broadcasted_iota(jnp.int32, (W, C), 0)
    before = jnp.where(column == 0, 0.0, pltpu.roll(row, 1, 0))
    after = jnp.where(column == W - 1, 0.0, pltpu.roll(row, W - 1, 0))
    for tap, part in enumerate((before, row, after)):
        dst[pair, :, pl.ds((half * 3 + tap) * C, C)] = part.astype(jnp.bfloat16)


def conv_pair(src, wide, slot, pair, emit):
    total = jnp.dot(
        src[pair], wide[slot, pl.ds(0, 6 * C), :], preferred_element_type=jnp.float32
    ) + jnp.dot(src[pair + 1], wide[slot, pl.ds(6 * C, 6 * C), :], preferred_element_type=jnp.float32)
    for half in range(2):
        emit(pair, half, total[:, half * C : (half + 1) * C])


def inner_steps(own, value_of, wide, mid, parts):
    values = {}
    for row in range(own):
        values[row] = value_of(row)
        spread(parts[0], row // 2, row % 2, values[row])
    for step in range(1, len(parts)):

        def hidden(pair, half, value, step=step):
            spread(parts[step], pair, half, jnp.tanh(value))

        def outer(pair, half, value, step=step):
            new = value_of(step + 2 * pair + half) + 0.5 * jnp.tanh(value)
            mid[2 * pair + half] = new
            spread(parts[step], pair, half, new)

        for pair in range(inner_pairs(own, step)):
            conv_pair(parts[step - 1], wide, step - 1, pair, outer if step % 2 == 0 else hidden)


def first_inner(own_ref, wide, mid, *parts):
    inner_steps(own_ref.shape[0], lambda row: own_ref[row], wide, mid, parts)


def second_inner(own_ref, wide, got_ref, begin_ref, mid, *parts):
    begin = lax.axis_index("depth") == 0
    for row in range(own_ref.shape[0]):
        begin_ref[row] = jnp.where(begin, own_ref[row], got_ref[row].astype(jnp.float32))
    inner_steps(own_ref.shape[0], lambda row: begin_ref[row], wide, mid, parts)


def third_inner(own_ref, wide, error_ref, begin_ref, mid, *parts):
    for row in range(own_ref.shape[0]):
        begin_ref[row] = own_ref[row] + error_ref[row].astype(jnp.float32)
    inner_steps(own_ref.shape[0], lambda row: begin_ref[row], wide, mid, parts)


def layers(count, halo, own, state, fields, wide, after_layer, mid, parts):
    slab = lax.axis_index("space")
    above = (slab > 0).astype(jnp.float32)
    below = (slab < lax.axis_size("space") - 1).astype(jnp.float32)

    def keep(row, value):
        if row < halo:
            return value * above
        if row >= halo + own:
            return value * below
        return value

    rows = own + 2 * halo
    for step in range(1, 2 * count + 1):
        src, dst = fields[(step - 1) % 2], fields[step % 2]
        inside = range(halo // 2, halo // 2 + inner_pairs(own, step))

        def hidden(pair, half, value, step=step, dst=dst):
            row = step + 2 * pair + half
            spread(dst, pair, half, keep(row, jnp.tanh(value)))

        def outer(pair, half, value, step=step, dst=dst):
            row = step + 2 * pair + half
            new = state[row] + 0.5 * keep(row, jnp.tanh(value))
            if step < 2 * count:
                state[row] = new
                spread(dst, pair, half, new)
            if halo <= row < halo + own:
                after_layer(step // 2, row - halo, new)

        for pair in range((rows - 2 * step) // 2):
            if pair not in inside:
                conv_pair(src, wide, step - 1, pair, outer if step % 2 == 0 else hidden)
                continue
            dst[pair] = parts[step][pair - halo // 2]
            if step % 2 == 0:
                for half in range(2):
                    row = step + 2 * pair + half
                    new = mid[2 * (pair - halo // 2) + half]
                    state[row] = new
                    after_layer(step // 2, row - halo, new)


def inner_pairs(own, step):
    return max(own // 2 - step, 0)


def load_rows(halo, own, value_of, state, field, part):
    for row in range(own + 2 * halo):
        value = value_of(row)
        state[row] = value
        if not halo <= row < halo + own:
            spread(field, row // 2, row % 2, value)
    for pair in range(own // 2):
        field[halo // 2 + pair] = part[pair]


def first_kernel(own_ref, wide, top_ref, bottom_ref, mid, *refs):
    parts, (y_ref, state, fa, fb) = refs[:-4], refs[-4:]
    own = own_ref.shape[0]
    halo = top_ref.shape[0]

    def value_of(row):
        if row < halo:
            return top_ref[row].astype(jnp.float32)
        if row >= halo + own:
            return bottom_ref[row - halo - own].astype(jnp.float32)
        return own_ref[row - halo]

    load_rows(halo, own, value_of, state, fa, parts[0])

    def after_layer(done, row, new):
        if 2 * done == halo:
            y_ref[row] = new.astype(jnp.bfloat16)

    layers(halo // 2, halo, own, state, (fa, fb), wide, after_layer, mid, parts)


def second_kernel(own_ref, wide, top_ref, bottom_ref, got_top_ref, got_bottom_ref, y_ref, mid, *refs):
    parts, (relaxed_ref, code_ref, state, fa, fb) = refs[:-5], refs[-5:]
    own = own_ref.shape[0]
    halo = top_ref.shape[0]
    begin = lax.axis_index("depth") == 0

    def value_of(row):
        if row < halo:
            return jnp.where(begin, top_ref[row], got_top_ref[row]).astype(jnp.float32)
        if row >= halo + own:
            at = row - halo - own
            return jnp.where(begin, bottom_ref[at], got_bottom_ref[at]).astype(jnp.float32)
        return own_ref[row - halo]

    load_rows(halo, own, value_of, state, fa, parts[0])

    def after_layer(done, row, new):
        if 2 * done == halo:
            relaxed_ref[row] = new
            resid = new - y_ref[row].astype(jnp.float32)
            code_ref[row] = encode(resid, RESID_SCALE)

    layers(halo // 2, halo, own, state, (fa, fb), wide, after_layer, mid, parts)


def third_kernel(own_ref, wide, top_ref, bottom_ref, got_top_ref, got_bottom_ref,
                 error_top_ref, error_bottom_ref, y_ref, mid, *refs):
    parts, (states_ref, relaxed_ref, state, fa, fb, kept, out_sems, relaxed_sem) = refs[:-8], refs[-8:]
    own = own_ref.shape[0]
    halo = error_top_ref.shape[0]
    skip = top_ref.shape[0] - halo
    begin = lax.axis_index("depth") == 0
    outs = [
        pltpu.make_async_copy(y_ref, relaxed_ref, relaxed_sem),
        pltpu.make_async_copy(own_ref, states_ref.at[0], out_sems.at[0, 0]),
    ]
    for out in outs:
        out.start()

    def put(done, row, value):
        kept[done, row] = value
        outs.append(
            pltpu.make_async_copy(
                kept.at[done, row], states_ref.at[done, row], out_sems.at[done, row]
            )
        )
        outs[-1].start()

    def value_of(row):
        if row < halo:
            value = jnp.where(begin, top_ref[row + skip], got_top_ref[row + skip])
            return value.astype(jnp.float32) + error_top_ref[row].astype(jnp.float32)
        if row >= halo + own:
            at = row - halo - own
            value = jnp.where(begin, bottom_ref[at], got_bottom_ref[at])
            return value.astype(jnp.float32) + error_bottom_ref[at].astype(jnp.float32)
        return own_ref[row - halo]

    load_rows(halo, own, value_of, state, fa, parts[0])
    layers(halo // 2, halo, own, state, (fa, fb), wide, put, mid, parts)
    for out in outs:
        out.wait()


def join_kernel(gain_ref, codes_ref, joined_ref):
    depth = lax.axis_index("depth")
    rows = joined_ref.shape[0]
    first = lax.rem(depth, 2) * rows
    later = lax.min(depth - lax.rem(depth, 2) + 2, gain_ref.shape[0] - 1)
    gain = gain_ref[pl.ds(later, 1), :]
    for row in range(rows):
        early = decode(codes_ref[0, first + row], RESID_SCALE)
        late = decode(codes_ref[1, first + row], RESID_SCALE)
        joined_ref[row] = encode(gain * early + late, JOINED_SCALE)


def scan_kernel(gain_ref, joined_ref, error_ref):
    count = error_ref.shape[0]
    carry = jnp.zeros(error_ref.shape[1:], jnp.float32)
    error_ref[0] = carry.astype(error_ref.dtype)
    for k in range(count - 1):
        gain = gain_ref[pl.ds(2 * k + 1, 1), :] * gain_ref[pl.ds(2 * k + 2, 1), :]
        carry = gain * carry + decode(joined_ref[k], JOINED_SCALE)
        error_ref[k + 1] = carry.astype(error_ref.dtype)


def split_kernel(gain_ref, codes_ref, pair_ref, error_ref, upper_ref, lower_ref):
    depth = lax.axis_index("depth")
    rows = error_ref.shape[0]
    near = upper_ref.shape[0]
    odd = lax.rem(depth, 2) == 1
    gain = gain_ref[pl.ds(depth, 1), :]
    for row in range(rows):
        error = pair_ref[row].astype(jnp.float32)
        own = gain * error + decode(codes_ref[0, row], RESID_SCALE)
        value = jnp.where(odd, own, error).astype(jnp.bfloat16)
        error_ref[row] = value
        if row < near:
            upper_ref[row] = value
        if row >= rows - near:
            lower_ref[row - rows + near] = value


def on_chip(count):
    return [pl.BlockSpec(memory_space=pltpu.VMEM)] * count


def small(kernel, outs, *args, flops=1):
    return pl.pallas_call(
        kernel,
        out_shape=outs,
        in_specs=on_chip(len(args)),
        out_specs=jax.tree.map(lambda _: on_chip(1)[0], outs),
        compiler_params=pltpu.CompilerParams(vmem_limit_bytes=VMEM_LIMIT),
        cost_estimate=pl.CostEstimate(
            flops=flops * 36 * C * C * W, bytes_accessed=2**19, transcendentals=0
        ),
    )(*args)


def sweep(kernel, halo, own, outs, args, kept=None):
    rows = own + 2 * halo
    scratch = [
        pltpu.VMEM((rows, W, C), jnp.float32),
        pltpu.VMEM((rows // 2, W, 6 * C), jnp.bfloat16),
        pltpu.VMEM((rows // 2, W, 6 * C), jnp.bfloat16),
    ]
    out_specs = on_chip(len(outs))
    if kept is not None:
        scratch += [
            pltpu.VMEM(outs[0].shape, jnp.float32),
            pltpu.SemaphoreType.DMA(kept),
            pltpu.SemaphoreType.DMA,
        ]
        out_specs = [pl.BlockSpec(memory_space=pltpu.HBM)] * len(outs)
    flops = 2 * 9 * C * C * W * sum(rows - 2 * k for k in range(1, halo + 1))
    return pl.pallas_call(
        kernel,
        out_shape=outs,
        in_specs=on_chip(len(args)),
        out_specs=tuple(out_specs),
        scratch_shapes=scratch,
        compiler_params=pltpu.CompilerParams(vmem_limit_bytes=VMEM_LIMIT),
        cost_estimate=pl.CostEstimate(flops=flops, bytes_accessed=2**22, transcendentals=0),
    )(*args)


def neighbour(block, up):
    count = lax.axis_size("space")
    route = [(i, i + 1) if up else (i + 1, i) for i in range(count - 1)]
    return lax.ppermute(block, "space", route)


def from_previous(block, shift):
    depth, space = lax.axis_size("depth"), lax.axis_size("space")
    route = [
        (d * space + s + shift, (d + 1) * space + s)
        for d in range(depth - 1)
        for s in range(space)
        if 0 <= s + shift < space
    ]
    return lax.ppermute(block, ("depth", "space"), route)


def shards(coarse_states, first_kernels, second_kernels, coarse_channel_gain):
    here = first_kernels.shape[0]
    start = coarse_states[0]
    own = start.shape[0]
    depth = lax.axis_size("depth")
    wide_field = jax.ShapeDtypeStruct(start.shape, jnp.float32)
    field = jax.ShapeDtypeStruct(start.shape, jnp.bfloat16)
    hbm = pl.BlockSpec(memory_space=pltpu.HBM)

    halo = 2 * here
    rounded = start.astype(jnp.bfloat16)
    top = neighbour(rounded[own - halo :], True)
    bottom = neighbour(rounded[:halo], False)
    start, wide = pl.pallas_call(
        taps_kernel,
        out_shape=(
            wide_field,
            jax.ShapeDtypeStruct((2 * here, 12 * C, 2 * C), jnp.bfloat16),
        ),
        in_specs=[hbm, hbm, hbm],
        out_specs=tuple(on_chip(2)),
        scratch_shapes=[pltpu.SemaphoreType.DMA((2 * here, 2)), pltpu.SemaphoreType.DMA],
        compiler_params=pltpu.CompilerParams(vmem_limit_bytes=VMEM_LIMIT),
        cost_estimate=pl.CostEstimate(flops=0, bytes_accessed=2**24, transcendentals=0),
    )(start, first_kernels.reshape(here, 9 * C, C), second_kernels.reshape(here, 9 * C, C))

    inner = [jax.ShapeDtypeStruct((own - 4,) + field.shape[1:], jnp.float32)] + [
        jax.ShapeDtypeStruct((inner_pairs(own, step), W, 6 * C), jnp.bfloat16)
        for step in range(own // 2)
    ]
    pairs_inside = sum(inner_pairs(own, step) for step in range(1, own // 2))
    known = small(first_inner, inner, start, wide, flops=pairs_inside)
    (y_first,) = sweep(first_kernel, halo, own, (field,), (start, wide, top, bottom, *known))
    got = from_previous(y_first, 0)
    got_top = from_previous(y_first[own - halo :], -1)
    got_bottom = from_previous(y_first[:halo], 1)
    begin, *known = small(second_inner, [wide_field] + inner, start, wide, got, flops=pairs_inside)
    y_second, code = sweep(
        second_kernel, halo, own, (wide_field, field),
        (begin, wide, top, bottom, got_top, got_bottom, y_first, *known),
    )
    pairs = [[at, at + 1] for at in range(0, depth, 2)]
    alike = [list(range(core, depth, 2)) for core in range(2)]
    codes = lax.all_gather(code, "depth", axis_index_groups=pairs)
    half = jax.ShapeDtypeStruct((own // 2,) + field.shape[1:], jnp.bfloat16)
    joined = small(join_kernel, half, coarse_channel_gain, codes)
    joined = joined.reshape(depth // 2, own * W // depth, C)
    joined = lax.all_to_all(joined, "depth", 0, 0, axis_index_groups=alike)
    errors = small(
        scan_kernel, jax.ShapeDtypeStruct(joined.shape, jnp.bfloat16), coarse_channel_gain, joined
    )
    errors = lax.all_to_all(errors, "depth", 0, 0, axis_index_groups=alike)
    pair = lax.all_gather(errors.reshape(half.shape), "depth", axis_index_groups=pairs)
    near = halo - 2
    part = jax.ShapeDtypeStruct((near,) + field.shape[1:], jnp.bfloat16)
    error, upper, lower = small(
        split_kernel, (field, part, part), coarse_channel_gain, codes, pair.reshape(field.shape)
    )
    error_top = neighbour(lower, True)
    error_bottom = neighbour(upper, False)
    begin, *known = small(
        third_inner, [wide_field] + inner, begin, wide, error, flops=pairs_inside
    )
    states, relaxed = sweep(
        third_kernel, near, own,
        (jax.ShapeDtypeStruct((here,) + start.shape, jnp.float32), wide_field),
        (begin, wide, top, bottom, got_top, got_bottom, error_top, error_bottom, y_second, *known),
        kept=(here, own),
    )
    return states, relaxed[None]


def solution(mesh):
    placed = (
        P("depth", "space", None, None),
        P("depth", None, None, None),
        P("depth", None, None, None),
        P(),
    )
    return jax.shard_map(
        shards,
        mesh=mesh,
        in_specs=placed,
        out_specs=(P("depth", "space", None, None), P("depth", "space", None, None)),
        check_vma=False,
    )
```
